256 devices in a mesh: grp: 16 (over z, x_hi), sp: 16 (over x_lo, y, core).
Axes of the slice: x: 4 (x_hi: 2, x_lo: 2; x = x_hi * 2 + x_lo), y: 4, z: 8, core: 2. Of those that a mesh axis runs over, the one named last changes fastest.
Arguments:
- queries: bfloat16 [16, 3072, 2048], P('grp', 'sp'), may hold values from -15 to 15
- keys: bfloat16 [16, 3072, 2048], P('grp', 'sp'), may hold values from -6 to 6
- values: bfloat16 [16, 3072, 2048], P('grp', 'sp'), may hold values from -6 to 6
- ref_cache: bfloat16 [16, 2, 2048, 2048], P('grp', None, 'sp'), may hold values from -6 to 6
- ref_ids: int32 [16], replicated, may hold values from 0 to 15
- ref_owner: int32 [16], replicated, may hold values from 0 to 15, each once
- ref_lens: int32 [16], replicated, may hold values from 256 to 2048, as said below
Outputs:
- attended: bfloat16 [16, 3072, 2048], P('grp', 'sp')
The draws below stay inside these ranges and needn't reach their ends.
Inputs may be any that keep to these rules, and one draw needn't show every extreme that they name: `ref_owner`: each reference image lies in exactly one cache row. `ref_lens`: some reference has 2048 live tokens and some 2048 // 8.
All inputs are finite; a program needn't handle non-finite values.
Results may differ from the reference program's by a relative error of at most 0.0031.
Values may be sent and summed in bfloat16 or wider, within the bound.
No kernel may reach another device: no remote copies, remote signals or barrier semaphores. Data moves between devices by JAX's collectives and lax.ppermute only.
A program may use at most 64 MiB of HBM per device.

```python
import math
import jax
import jax.numpy as jnp
import numpy as np
from jax import lax

HEADS = 16
HEAD_DIM = 128
ATTN_WIDTH = 2048
SEQ = 3072
REF_LEN = 2048
N_GRP = 16


def draw_queries(key, part):
    key = jax.random.fold_in(key, 11)
    shape_all = (N_GRP, SEQ, HEADS * HEAD_DIM)
    base = jnp.clip(2.5 * jax.random.normal(key, shape_all, jnp.float32), -15.0, 15.0)
    return base.astype(jnp.bfloat16)


def draw_keys(key, part):
    key = jax.random.fold_in(key, 12)
    shape_all = (N_GRP, SEQ, HEADS * HEAD_DIM)
    base = jnp.clip(jax.random.normal(key, shape_all, jnp.float32), -6.0, 6.0)
    return base.astype(jnp.bfloat16)


def draw_ref_lens(key, part):
    key = jax.random.fold_in(key, 13)
    first_key, second_key = jax.random.split(key)
    lengths = jax.random.randint(first_key, (N_GRP,), REF_LEN // 8, REF_LEN + 1)
    order = jax.random.permutation(second_key, N_GRP)
    lengths = lengths.at[order[0]].set(REF_LEN).at[order[1]].set(REF_LEN // 8)
    return lengths.astype(jnp.int32)


def place_ends(result, rng, least, top_value):
    dims = result.shape
    place = [jax.random.randint(jax.random.fold_in(rng, axis), (), 0, dims[axis]) for axis in range(len(dims))]
    result = result.at[tuple(place)].set(least)
    longest = dims.index(max(dims))
    place[longest] = (place[longest] + 1) % dims[longest]
    return result.at[tuple(place)].set(top_value)


def steps_of(key, dims, pieces, least, largest):
    level, own = 1.0, jax.random.fold_in(key, 6)
    for position, blocks in pieces:
        heights = jnp.exp(jax.random.uniform(jax.random.fold_in(own, position), (blocks,), jnp.float32, least / len(pieces), largest / len(pieces)))
        level = level * jnp.repeat(heights, dims[position] // blocks).reshape([-1 if axis == position else 1 for axis in range(len(dims))])
    return level


def cumulative_ranks(number_of, skew):
    weights = [(1 << 20) // math.isqrt(grade ** skew) + 1 for grade in range(1, number_of + 1)]
    deviation = 1 + sum(weights) // (1 << 30)
    return np.cumsum(np.array([max(1, weight // deviation) for weight in weights]))


def ranked_ids(key, dims, count, slope):
    grid = cumulative_ranks(count, slope)
    ticket = jax.random.randint(jax.random.fold_in(key, 1), dims, 0, int(grid[count - 1]))
    rank = jnp.searchsorted(jnp.asarray(grid, jnp.int32), ticket, side="right")
    return jax.random.permutation(jax.random.fold_in(key, 2), count)[rank].astype(jnp.int32)


def scatter_about(own_key, shape, deviation, most, cuts=(), kind=jnp.bfloat16):
    entries = deviation * jax.random.normal(own_key, shape, jnp.float32)
    if cuts:
        entries = entries * steps_of(own_key, shape, cuts, -0.22, 0.18)
    return jnp.clip(entries, -most, most).astype(kind)


def setup_inputs(seed: int = 0) -> dict:
    streams_of = jax.random.split(jax.random.key(seed), 8)
    queries = draw_queries(jax.random.fold_in(streams_of[7], 71), 0)
    keys = draw_keys(jax.random.fold_in(streams_of[7], 71), 0)
    values = scatter_about(streams_of[2], (N_GRP, SEQ, ATTN_WIDTH), 1.0, 6.0, ((0, 16), (1, 16)))
    ref_cache = scatter_about(streams_of[3], (N_GRP, 2, REF_LEN, ATTN_WIDTH), 1.0, 6.0, ((0, 16), (2, 16)))
    ref_ids = place_ends(ranked_ids(streams_of[4], (N_GRP,), N_GRP, 2), jax.random.fold_in(streams_of[4], 3), 0, N_GRP - 1).astype(jnp.int32)
    ref_owner = jax.random.permutation(streams_of[5], N_GRP).astype(jnp.int32)
    ref_lens = draw_ref_lens(jax.random.fold_in(streams_of[7], 71), 0)
    return {"queries": queries, "keys": keys, "values": values, "ref_cache": ref_cache, "ref_ids": ref_ids, "ref_owner": ref_owner, "ref_lens": ref_lens}


def reference(queries, keys, values, ref_cache, ref_ids, ref_owner, ref_lens):
    wanted_row = ref_owner[ref_ids].astype(jnp.int32)
    ref_live = ref_lens[ref_ids].astype(jnp.int32)
    score_scale = HEAD_DIM ** -0.5

    def one_group(group_idx):
        cache_row = lax.dynamic_index_in_dim(ref_cache, wanted_row[group_idx], 0, keepdims=False)
        key_set = jnp.concatenate([keys[group_idx], cache_row[0]], axis=0)
        value_set = jnp.concatenate([values[group_idx], cache_row[1]], axis=0)
        live_mask = jnp.arange(SEQ + REF_LEN, dtype=jnp.int32) < SEQ + ref_live[group_idx]
        own_queries = queries[group_idx]

        def one_head(head_idx):
            start = (head_idx * HEAD_DIM).astype(jnp.int32)
            q_head = lax.dynamic_slice_in_dim(own_queries, start, HEAD_DIM, 1)
            k_head = lax.dynamic_slice_in_dim(key_set, start, HEAD_DIM, 1)
            v_head = lax.dynamic_slice_in_dim(value_set, start, HEAD_DIM, 1)
            scores = jnp.dot(q_head, k_head.T, preferred_element_type=jnp.float32) * score_scale
            scores = jnp.where(live_mask[None, :], scores, -jnp.inf)
            row_peak = jnp.max(scores, axis=-1, keepdims=True)
            weights = jnp.exp(scores - row_peak)
            row_total = jnp.sum(weights, axis=-1, keepdims=True)
            soft_probs = weights.astype(jnp.bfloat16)
            mixed_out = jnp.dot(soft_probs, v_head, preferred_element_type=jnp.float32)
            return (mixed_out / row_total).astype(jnp.bfloat16)

        head_outs = lax.map(one_head, jnp.arange(HEADS, dtype=jnp.int32))
        return jnp.transpose(head_outs, (1, 0, 2)).reshape(SEQ, HEADS * HEAD_DIM)

    return lax.map(one_group, jnp.arange(N_GRP, dtype=jnp.int32))
```

```python
import functools
import math

import jax
import jax.numpy as jnp
from jax import lax
from jax.experimental import pallas as pl
from jax.experimental.pallas import tpu as pltpu
from jax.sharding import PartitionSpec as P

D = 128
EXP_SCALE = D**-0.5 * math.log2(math.e)
ROWS_CONTRACT = (((1,), (1,)), ((), ()))
VMEM_LIMIT = 48 << 20


def params():
    return pltpu.CompilerParams(vmem_limit_bytes=VMEM_LIMIT)


def whole(memory_space=pltpu.VMEM):
    return pl.BlockSpec(memory_space=memory_space)


def pack_kernel(q_ref, k_ref, v_ref, out_ref):
    for head in range(out_ref.shape[0]):
        cols = slice(head * D, (head + 1) * D)
        for which, ref in enumerate((q_ref, k_ref, v_ref)):
            out_ref[head, which] = ref[:, cols]


def pack_heads(q, k, v):
    tokens, width = q.shape
    heads = width // D
    size = 2 * q.size * q.dtype.itemsize * 3
    return pl.pallas_call(
        pack_kernel,
        in_specs=[whole()] * 3,
        out_specs=whole(),
        out_shape=jax.ShapeDtypeStruct((heads, 3, tokens, D), q.dtype),
        compiler_params=params(),
        cost_estimate=pl.CostEstimate(flops=0, bytes_accessed=size, transcendentals=0),
        name="pack_heads",
    )(q, k, v)


def route_kernel(ids_ref, owner_ref, held_ref, out_ref):
    groups, heads = out_ref.shape[:2]
    for group in range(groups):
        row = owner_ref[ids_ref[group]]
        for head in range(heads):
            out_ref[group, head] = held_ref[row, :, head * D : (head + 1) * D]


def route_pieces(ids, owner, held):
    rows, tokens, width = held.shape
    groups = ids.shape[0]
    heads = width // D
    return pl.pallas_call(
        route_kernel,
        in_specs=[whole(pltpu.SMEM), whole(pltpu.SMEM), whole()],
        out_specs=whole(),
        out_shape=jax.ShapeDtypeStruct((groups, heads, tokens, D), held.dtype),
        compiler_params=params(),
        cost_estimate=pl.CostEstimate(
            flops=0, bytes_accessed=2 * held.size * 2, transcendentals=0
        ),
        name="route_pieces",
    )(ids, owner, held)


def unpack_kernel(x_ref, out_ref):
    for head in range(x_ref.shape[0]):
        out_ref[:, head * D : (head + 1) * D] = x_ref[head]


def unpack_heads(x):
    heads, tokens, _ = x.shape
    return pl.pallas_call(
        unpack_kernel,
        in_specs=[whole()],
        out_specs=whole(),
        out_shape=jax.ShapeDtypeStruct((tokens, heads * D), x.dtype),
        compiler_params=params(),
        name="unpack_heads",
    )(x)


def attend_block(q, k, v_ones, state):
    s = lax.dot_general(q, k, ROWS_CONTRACT, preferred_element_type=jnp.float32)
    peak = jnp.max(s, axis=1, keepdims=True)
    if state is not None:
        peak = jnp.maximum(state[1], peak)
    p = jnp.exp2((s - peak) * EXP_SCALE).astype(jnp.bfloat16)
    part = jnp.dot(p, v_ones, preferred_element_type=jnp.float32)
    if state is not None:
        part = state[0] * jnp.exp2((state[1] - peak) * EXP_SCALE) + part
    return part, peak


def own_kernel(q_ref, k_ref, v_ref, acc_ref, peak_ref, *, rows, sub, steps):
    shards, tokens, _ = k_ref.shape
    per = shards // steps
    q_all = q_ref[...].reshape(rows, D)
    for start in range(0, rows, sub):
        q = q_all[start : start + sub]
        state = None
        for step in range(steps):
            k = k_ref[step * per : (step + 1) * per].reshape(per * tokens, D)
            v = v_ref[step * per : (step + 1) * per].reshape(per * tokens, D)
            v_ones = jnp.concatenate([v, jnp.ones_like(v)], axis=1)
            state = attend_block(q, k, v_ones, state)
        acc_ref[start : start + sub] = state[0]
        peak_ref[start : start + sub] = jnp.broadcast_to(state[1], (sub, D))


def attend_own(qkv):
    shards, _, tokens, _ = qkv.shape
    n = shards * tokens
    rows, sub = 4 * tokens, tokens
    return pl.pallas_call(
        functools.partial(own_kernel, rows=rows, sub=sub, steps=4),
        grid=(n // rows,),
        in_specs=[
            pl.BlockSpec((rows // tokens, None, tokens, D), lambda i: (i, 0, 0, 0)),
            pl.BlockSpec((shards, None, tokens, D), lambda i: (0, 1, 0, 0)),
            pl.BlockSpec((shards, None, tokens, D), lambda i: (0, 2, 0, 0)),
        ],
        out_specs=[
            pl.BlockSpec((rows, 2 * D), lambda i: (i, 0)),
            pl.BlockSpec((rows, D), lambda i: (i, 0)),
        ],
        out_shape=[
            jax.ShapeDtypeStruct((n, 2 * D), jnp.float32),
            jax.ShapeDtypeStruct((n, D), jnp.float32),
        ],
        compiler_params=params(),
        cost_estimate=pl.CostEstimate(
            flops=8 * n * n * D, bytes_accessed=12 * n * D, transcendentals=n * n
        ),
        name="attend_own",
    )(qkv, qkv, qkv)


def ref_kernel(
    live_ref, q_ref, acc_ref, peak_ref, kv_ref, out_ref, k_held, v_held, *, rows, sub, steps
):
    halves, pieces, shards, tokens, _ = kv_ref.shape
    n_keys = pieces * shards * tokens
    block = n_keys // steps

    @pl.when(pl.program_id(0) == 0)
    def _():
        place = lax.broadcasted_iota(jnp.int32, (n_keys, D), 0)
        piece = place // (shards * tokens)
        shard = place // tokens % shards
        position = (shard * pieces + piece) * tokens + place % tokens
        live = position < live_ref[0]
        k = kv_ref[0].reshape(n_keys, D).astype(jnp.float32)
        v = kv_ref[1].reshape(n_keys, D).astype(jnp.float32)
        k_held[...] = jnp.where(live, k, k[:1]).astype(jnp.bfloat16)
        v_held[:, :D] = jnp.where(live, v, 0.0).astype(jnp.bfloat16)
        v_held[:, D:] = jnp.where(live, 1.0, 0.0).astype(jnp.bfloat16)

    q_all = q_ref[...].reshape(rows, D)
    for start in range(0, rows, sub):
        here = slice(start, start + sub)
        state = (acc_ref[here], peak_ref[here, :1])
        for step in range(steps):
            keys = slice(step * block, (step + 1) * block)
            state = attend_block(q_all[here], k_held[keys], v_held[keys], state)
        out_ref[here] = (state[0][:, :D] / state[0][:, D:]).astype(jnp.bfloat16)


def attend_ref(qkv, acc, peak, kv, live):
    shards, _, tokens, _ = qkv.shape
    n = shards * tokens
    rows, sub = 4 * tokens, tokens
    n_keys = kv.size // (2 * D)
    return pl.pallas_call(
        functools.partial(ref_kernel, rows=rows, sub=sub, steps=2),
        grid=(n // rows,),
        in_specs=[
            whole(pltpu.SMEM),
            pl.BlockSpec((rows // tokens, None, tokens, D), lambda i: (i, 0, 0, 0)),
            pl.BlockSpec((rows, 2 * D), lambda i: (i, 0)),
            pl.BlockSpec((rows, D), lambda i: (i, 0)),
            pl.BlockSpec(kv.shape, lambda i: (0,) * kv.ndim),
        ],
        out_specs=pl.BlockSpec((rows, D), lambda i: (i, 0)),
        out_shape=jax.ShapeDtypeStruct((n, D), jnp.bfloat16),
        scratch_shapes=[
            pltpu.VMEM((n_keys, D), jnp.bfloat16),
            pltpu.VMEM((n_keys, 2 * D), jnp.bfloat16),
        ],
        compiler_params=params(),
        cost_estimate=pl.CostEstimate(
            flops=8 * n * n_keys * D, bytes_accessed=16 * n * D, transcendentals=n * n_keys
        ),
        name="attend_ref",
    )(live, qkv, acc, peak, kv)


def swap(x, axes):
    return lax.all_to_all(x, axes, split_axis=0, concat_axis=0, tiled=True)


def shards(n_grp, n_sp, queries, keys, values, ref_cache, ref_ids, ref_owner, ref_lens):
    live = ref_lens[ref_ids[lax.axis_index("grp")]].reshape(1)

    cache = ref_cache[0]
    width = cache.shape[-1]
    tokens = 2 * cache.shape[1] // n_grp
    held = swap(cache.reshape(n_grp, tokens, width), "grp")

    qkv = swap(pack_heads(queries[0], keys[0], values[0]), "sp")

    routed = route_pieces(ref_ids, ref_owner, held)
    routed = swap(routed.reshape(n_grp * n_sp, tokens, D), ("grp", "sp"))
    kv = routed.reshape(2, n_grp // 2, n_sp, tokens, D)

    acc, peak = attend_own(qkv)
    out = attend_ref(qkv, acc, peak, kv, live)

    back = swap(out.reshape(n_sp, -1, D), "sp")
    return unpack_heads(back)[None]


def solution(mesh):
    in_specs = (
        P("grp", "sp", None),
        P("grp", "sp", None),
        P("grp", "sp", None),
        P("grp", None, "sp", None),
        P(),
        P(),
        P(),
    )
    body = functools.partial(shards, mesh.shape["grp"], mesh.shape["sp"])
    return jax.shard_map(
        body, mesh=mesh, in_specs=in_specs, out_specs=P("grp", "sp", None), check_vma=False
    )
```

```python
import functools
import math

import jax
import jax.numpy as jnp
from jax import lax
from jax.experimental import pallas as pl
from jax.experimental.pallas import tpu as pltpu
from jax.sharding import PartitionSpec as P

D = 128
EXP_SCALE = D**-0.5 * math.log2(math.e)
ROWS_CONTRACT = (((1,), (1,)), ((), ()))
VMEM_LIMIT = 48 << 20


def params():
    return pltpu.CompilerParams(vmem_limit_bytes=VMEM_LIMIT)


def whole(memory_space=pltpu.VMEM):
    return pl.BlockSpec(memory_space=memory_space)


def pack_kernel(q_ref, k_ref, v_ref, out_ref):
    for head in range(out_ref.shape[0]):
        cols = slice(head * D, (head + 1) * D)
        for which, ref in enumerate((q_ref, k_ref, v_ref)):
            out_ref[head, which] = ref[:, cols]


def pack_heads(q, k, v):
    tokens, width = q.shape
    heads = width // D
    size = 2 * q.size * q.dtype.itemsize * 3
    return pl.pallas_call(
        pack_kernel,
        in_specs=[whole()] * 3,
        out_specs=whole(),
        out_shape=jax.ShapeDtypeStruct((heads, 3, tokens, D), q.dtype),
        compiler_params=params(),
        cost_estimate=pl.CostEstimate(flops=0, bytes_accessed=size, transcendentals=0),
        name="pack_heads",
    )(q, k, v)


def spread_kernel(n_z, place_ref, cache_ref, other_ref, *out_refs):
    z, x = place_ref[0], place_ref[1]
    tokens = out_refs[0].shape[1]
    for shift, out_ref in enumerate(out_refs):
        rows = pl.ds(pl.multiple_of((z + shift) % n_z * tokens, tokens), tokens)
        out_ref[0] = cache_ref[x, rows]
        out_ref[1] = other_ref[rows]


def spread_pieces(n_z, place, cache, other):
    _, rows, width = cache.shape
    piece = jax.ShapeDtypeStruct((2, rows // n_z, width), cache.dtype)
    return pl.pallas_call(
        functools.partial(spread_kernel, n_z),
        in_specs=[whole(pltpu.SMEM), whole(), whole()],
        out_specs=[whole()] * n_z,
        out_shape=[piece] * n_z,
        compiler_params=params(),
        cost_estimate=pl.CostEstimate(flops=0, bytes_accessed=8 * rows * width, transcendentals=0),
        name="spread_pieces",
    )(place, cache, other)


def route_kernel(n_z, place_ref, ids_ref, owner_ref, *refs):
    held_refs, out_ref, held = refs[:n_z], refs[-2], refs[-1]
    z, x = place_ref[0], place_ref[1]
    for shift, ref in enumerate(held_refs):
        held[shift] = ref[...]
    for group in range(out_ref.shape[0]):
        row = owner_ref[ids_ref[group]]
        shift, side = (z - row // 2 + n_z) % n_z, (row + x) % 2
        for head in range(out_ref.shape[1]):
            out_ref[group, head] = held[shift, side, :, head * D : (head + 1) * D]


def route_pieces(n_z, place, ids, owner, pieces):
    piece = pieces[0]
    _, tokens, width = piece.shape
    return pl.pallas_call(
        functools.partial(route_kernel, n_z),
        in_specs=[whole(pltpu.SMEM)] * 3 + [whole()] * n_z,
        out_specs=whole(),
        out_shape=jax.ShapeDtypeStruct((2 * n_z, width // D, tokens, D), piece.dtype),
        scratch_shapes=[pltpu.VMEM((n_z, *piece.shape), piece.dtype)],
        compiler_params=params(),
        cost_estimate=pl.CostEstimate(
            flops=0, bytes_accessed=4 * n_z * piece.size, transcendentals=0
        ),
        name="route_pieces",
    )(place, ids, owner, *pieces)


def unpack_kernel(x_ref, out_ref):
    for head in range(x_ref.shape[0]):
        out_ref[:, head * D : (head + 1) * D] = x_ref[head]


def unpack_heads(x):
    heads, tokens, _ = x.shape
    return pl.pallas_call(
        unpack_kernel,
        in_specs=[whole()],
        out_specs=whole(),
        out_shape=jax.ShapeDtypeStruct((tokens, heads * D), x.dtype),
        compiler_params=params(),
        name="unpack_heads",
    )(x)


def attend_block(q, k, v_ones, state):
    s = lax.dot_general(q, k, ROWS_CONTRACT, preferred_element_type=jnp.float32)
    peak = jnp.max(s, axis=1, keepdims=True)
    if state is not None:
        peak = jnp.maximum(state[1], peak)
    p = jnp.exp2((s - peak) * EXP_SCALE).astype(jnp.bfloat16)
    part = jnp.dot(p, v_ones, preferred_element_type=jnp.float32)
    if state is not None:
        part = state[0] * jnp.exp2((state[1] - peak) * EXP_SCALE) + part
    return part, peak


def own_kernel(q_ref, k_ref, v_ref, acc_ref, peak_ref, *, rows, sub, steps):
    shards, tokens, _ = k_ref.shape
    per = shards // steps
    q_all = q_ref[...].reshape(rows, D)
    for start in range(0, rows, sub):
        q = q_all[start : start + sub]
        state = None
        for step in range(steps):
            k = k_ref[step * per : (step + 1) * per].reshape(per * tokens, D)
            v = v_ref[step * per : (step + 1) * per].reshape(per * tokens, D)
            v_ones = jnp.concatenate([v, jnp.ones_like(v)], axis=1)
            state = attend_block(q, k, v_ones, state)
        acc_ref[start : start + sub] = state[0]
        peak_ref[start : start + sub] = jnp.broadcast_to(state[1], (sub, D))


def attend_own(qkv):
    shards, _, tokens, _ = qkv.shape
    n = shards * tokens
    rows, sub = 4 * tokens, tokens
    return pl.pallas_call(
        functools.partial(own_kernel, rows=rows, sub=sub, steps=4),
        grid=(n // rows,),
        in_specs=[
            pl.BlockSpec((rows // tokens, None, tokens, D), lambda i: (i, 0, 0, 0)),
            pl.BlockSpec((shards, None, tokens, D), lambda i: (0, 1, 0, 0)),
            pl.BlockSpec((shards, None, tokens, D), lambda i: (0, 2, 0, 0)),
        ],
        out_specs=[
            pl.BlockSpec((rows, 2 * D), lambda i: (i, 0)),
            pl.BlockSpec((rows, D), lambda i: (i, 0)),
        ],
        out_shape=[
            jax.ShapeDtypeStruct((n, 2 * D), jnp.float32),
            jax.ShapeDtypeStruct((n, D), jnp.float32),
        ],
        compiler_params=params(),
        cost_estimate=pl.CostEstimate(
            flops=8 * n * n * D, bytes_accessed=12 * n * D, transcendentals=n * n
        ),
        name="attend_own",
    )(qkv, qkv, qkv)


def ref_kernel(
    live_ref, q_ref, acc_ref, peak_ref, kv_ref, out_ref, k_held, v_held, *, rows, sub, steps
):
    pieces, _, shards, tokens, _ = kv_ref.shape
    n_keys = pieces * shards * tokens
    block = n_keys // steps

    @pl.when(pl.program_id(0) == 0)
    def _():
        place = lax.broadcasted_iota(jnp.int32, (n_keys, D), 0)
        piece = place // (shards * tokens)
        shard = place // tokens % shards
        position = (shard * pieces + piece) * tokens + place % tokens
        live = position < live_ref[0]
        k = kv_ref[:, 0].reshape(n_keys, D).astype(jnp.float32)
        v = kv_ref[:, 1].reshape(n_keys, D).astype(jnp.float32)
        k_held[...] = jnp.where(live, k, k[:1]).astype(jnp.bfloat16)
        v_held[:, :D] = jnp.where(live, v, 0.0).astype(jnp.bfloat16)
        v_held[:, D:] = jnp.where(live, 1.0, 0.0).astype(jnp.bfloat16)

    q_all = q_ref[...].reshape(rows, D)
    for start in range(0, rows, sub):
        here = slice(start, start + sub)
        state = (acc_ref[here], peak_ref[here, :1])
        for step in range(steps):
            keys = slice(step * block, (step + 1) * block)
            state = attend_block(q_all[here], k_held[keys], v_held[keys], state)
        out_ref[here] = (state[0][:, :D] / state[0][:, D:]).astype(jnp.bfloat16)


def attend_ref(qkv, acc, peak, kv, live):
    shards, _, tokens, _ = qkv.shape
    n = shards * tokens
    rows, sub = 4 * tokens, tokens
    n_keys = kv.size // (2 * D)
    return pl.pallas_call(
        functools.partial(ref_kernel, rows=rows, sub=sub, steps=2),
        grid=(n // rows,),
        in_specs=[
            whole(pltpu.SMEM),
            pl.BlockSpec((rows // tokens, None, tokens, D), lambda i: (i, 0, 0, 0)),
            pl.BlockSpec((rows, 2 * D), lambda i: (i, 0)),
            pl.BlockSpec((rows, D), lambda i: (i, 0)),
            pl.BlockSpec(kv.shape, lambda i: (0,) * kv.ndim),
        ],
        out_specs=pl.BlockSpec((rows, D), lambda i: (i, 0)),
        out_shape=jax.ShapeDtypeStruct((n, D), jnp.bfloat16),
        scratch_shapes=[
            pltpu.VMEM((n_keys, D), jnp.bfloat16),
            pltpu.VMEM((n_keys, 2 * D), jnp.bfloat16),
        ],
        compiler_params=params(),
        cost_estimate=pl.CostEstimate(
            flops=8 * n * n_keys * D, bytes_accessed=16 * n * D, transcendentals=n * n_keys
        ),
        name="attend_ref",
    )(live, qkv, acc, peak, kv)


def swap(x, axes):
    return lax.all_to_all(x, axes, split_axis=0, concat_axis=0, tiled=True)


def shift_all(pieces, n_z):
    moved = list(pieces)
    for shift in sorted(range(1, n_z), key=lambda s: -min(s, n_z - s)):
        pairs = [(src, (src + shift) % n_z) for src in range(n_z)]
        moved[shift] = lax.ppermute(pieces[shift], "z", pairs)
    return moved


def shards(n_z, queries, keys, values, ref_cache, ref_ids, ref_owner, ref_lens):
    z, x = lax.axis_index("z"), lax.axis_index("x")
    place = jnp.stack([z, x]).astype(jnp.int32)
    live = ref_lens[ref_ids[2 * z + x]].reshape(1)

    cache = ref_cache[0]
    other = lax.ppermute(lax.dynamic_index_in_dim(cache, 1 - x, 0, keepdims=False), "x", [(0, 1), (1, 0)])

    packed, other = lax.optimization_barrier((pack_heads(queries[0], keys[0], values[0]), other))
    qkv = swap(packed, "sp")

    held = shift_all(spread_pieces(n_z, place, cache, other), n_z)
    routed = route_pieces(n_z, place, ref_ids, ref_owner, held)
    tokens = routed.shape[2]
    kv = swap(routed.reshape(-1, tokens, D), ("z", "x", "sp")).reshape(n_z, 2, -1, tokens, D)

    acc, peak = attend_own(qkv)
    out = attend_ref(qkv, acc, peak, kv, live)

    back = swap(out.reshape(qkv.shape[0], -1, D), "sp")
    return unpack_heads(back)[None]


def solution(mesh):
    n_grp, n_sp = mesh.devices.shape
    n_z = n_grp // 2
    split = jax.sharding.Mesh(mesh.devices.reshape(n_z, 2, n_sp), ("z", "x", "sp"))
    token_spec = P(("z", "x"), "sp", None)
    return jax.shard_map(
        functools.partial(shards, n_z),
        mesh=split,
        in_specs=(token_spec,) * 3 + (P(("z", "x"), None, "sp", None), P(), P(), P()),
        out_specs=token_spec,
        check_vma=False,
    )
```

```python
import functools
import math

import jax
import jax.numpy as jnp
from jax import lax
from jax.experimental import pallas as pl
from jax.experimental.pallas import tpu as pltpu
from jax.sharding import PartitionSpec as P

D = 128
EXP_SCALE = D**-0.5 * math.log2(math.e)
ROWS_CONTRACT = (((1,), (1,)), ((), ()))
VMEM_LIMIT = 24 << 20
PER_ROW = 8


def params():
    return pltpu.CompilerParams(vmem_limit_bytes=VMEM_LIMIT)


def whole(memory_space=pltpu.VMEM):
    return pl.BlockSpec(memory_space=memory_space)


def pack_kernel(q_ref, k_ref, v_ref, out_ref):
    for head in range(out_ref.shape[0]):
        cols = slice(head * D, (head + 1) * D)
        for which, ref in enumerate((q_ref, k_ref, v_ref)):
            out_ref[head, which] = ref[:, cols]


def pack_heads(q, k, v):
    tokens, width = q.shape
    heads = width // D
    return pl.pallas_call(
        pack_kernel,
        in_specs=[whole()] * 3,
        out_specs=whole(),
        out_shape=jax.ShapeDtypeStruct((heads, 3, tokens, D), q.dtype),
        compiler_params=params(),
        cost_estimate=pl.CostEstimate(flops=0, bytes_accessed=12 * q.size, transcendentals=0),
        name="pack_heads",
    )(q, k, v)


def spread_kernel(n_z, shifts, place_ref, cache_ref, other_ref, *out_refs):
    z, x = place_ref[0], place_ref[1]
    for shift, out_ref in zip(shifts, out_refs):
        tokens = out_ref.shape[1]
        here = pl.ds(pl.multiple_of((z + shift) % n_z * tokens, tokens), tokens)
        out_ref[0] = cache_ref[x, here]
        out_ref[1] = other_ref[here]


def spread_pieces(n_z, place, shifts, cache, other):
    piece = jax.ShapeDtypeStruct((2, cache.shape[1] // n_z, cache.shape[2]), cache.dtype)
    return pl.pallas_call(
        functools.partial(spread_kernel, n_z, shifts),
        in_specs=[whole(pltpu.SMEM), whole(), whole()],
        out_specs=[whole()] * n_z,
        out_shape=[piece] * n_z,
        compiler_params=params(),
        cost_estimate=pl.CostEstimate(flops=0, bytes_accessed=4 * cache.size, transcendentals=0),
        name="spread_pieces",
    )(place, cache, other)


def route_kernel(n_z, shifts, place_ref, ids_ref, owner_ref, *refs):
    out_ref, held = refs[-2:]
    z, x = place_ref[0], place_ref[1]
    for shift, ref in zip(shifts, refs[:-2]):
        held[shift] = ref[0]
        held[n_z + shift] = ref[1]
    for group in range(out_ref.shape[0]):
        row = owner_ref[ids_ref[group]]
        slot = (row + x) % 2 * n_z + (z - row // 2 + n_z) % n_z
        for head in range(out_ref.shape[1]):
            out_ref[group, head] = held[slot, :, head * D : (head + 1) * D]


def route_pieces(n_z, place, ids, owner, pieces, shifts):
    _, tokens, width = pieces[0].shape
    return pl.pallas_call(
        functools.partial(route_kernel, n_z, shifts),
        in_specs=[whole(pltpu.SMEM)] * 3 + [whole()] * len(pieces),
        out_specs=whole(),
        out_shape=jax.ShapeDtypeStruct((2 * n_z, width // D, tokens, D), pieces[0].dtype),
        scratch_shapes=[pltpu.VMEM((2 * n_z, tokens, width), pieces[0].dtype)],
        compiler_params=params(),
        cost_estimate=pl.CostEstimate(
            flops=0, bytes_accessed=8 * n_z * tokens * width, transcendentals=0
        ),
        name="route_pieces",
    )(place, ids, owner, *pieces)


def unpack_kernel(x_ref, out_ref):
    for head in range(x_ref.shape[0]):
        out_ref[:, head * D : (head + 1) * D] = x_ref[head]


def unpack_heads(x):
    heads, tokens, _ = x.shape
    return pl.pallas_call(
        unpack_kernel,
        in_specs=[whole()],
        out_specs=whole(),
        out_shape=jax.ShapeDtypeStruct((tokens, heads * D), x.dtype),
        compiler_params=params(),
        name="unpack_heads",
    )(x)


def attend_block(q, k, v_ones, state):
    s = lax.dot_general(q, k, ROWS_CONTRACT, preferred_element_type=jnp.float32)
    peak = jnp.max(s, axis=1, keepdims=True)
    if state is not None:
        peak = jnp.maximum(state[1], peak)
    p = jnp.exp2((s - peak) * EXP_SCALE).astype(jnp.bfloat16)
    part = jnp.dot(p, v_ones, preferred_element_type=jnp.float32)
    if state is not None:
        part = state[0] * jnp.exp2((state[1] - peak) * EXP_SCALE) + part
    return part, peak


def own_kernel(qkv_ref, acc_ref, stats_ref, *, per_row, steps):
    shards, _, tokens, _ = qkv_ref.shape
    per = shards // steps
    base = pl.program_id(0) * per_row
    for i in range(per_row):
        q = qkv_ref[base + i, 0]
        state = None
        for step in range(steps):
            here = slice(step * per, (step + 1) * per)
            k = qkv_ref[here, 1].reshape(per * tokens, D)
            v = qkv_ref[here, 2].reshape(per * tokens, D)
            v_ones = jnp.concatenate([v, jnp.ones_like(v)], axis=1)
            state = attend_block(q, k, v_ones, state)
        acc_ref[base + i] = state[0][:, :D]
        column = lax.broadcasted_iota(jnp.int32, (tokens, D), 1)
        stats = jnp.where(column == 0, state[0][:, D:], state[1])
        stats_ref[base + i] = jnp.transpose(stats)[: stats_ref.shape[1]]


def attend_own(qkv):
    shards, _, tokens, _ = qkv.shape
    n = shards * tokens
    return pl.pallas_call(
        functools.partial(own_kernel, per_row=PER_ROW, steps=4),
        grid=(shards // PER_ROW,),
        in_specs=[whole()],
        out_specs=[whole()] * 2,
        out_shape=[
            jax.ShapeDtypeStruct((shards, tokens, D), jnp.float32),
            jax.ShapeDtypeStruct((shards, 8, tokens), jnp.float32),
        ],
        compiler_params=params(),
        cost_estimate=pl.CostEstimate(
            flops=8 * n * n * D, bytes_accessed=12 * n * D, transcendentals=n * n
        ),
        name="attend_own",
    )(qkv)


def ref_kernel(
    live_ref, qkv_ref, acc_ref, stats_ref, kv_ref, out_ref, k_held, v_held, *, per_row, steps
):
    pieces, _, shards, tokens, _ = kv_ref.shape
    n_keys = pieces * shards * tokens
    block = n_keys // steps

    @pl.when(pl.program_id(0) == 0)
    def _():
        for piece in range(pieces):
            for shard in range(shards):
                start = (shard * pieces + piece) * tokens
                k_held[start : start + tokens] = kv_ref[piece, 0, shard]
                v_held[start : start + tokens, :D] = kv_ref[piece, 1, shard]
        v_held[:, D:] = jnp.ones((n_keys, D), jnp.bfloat16)

        for start in range(0, n_keys, block):
            keys = slice(start, start + block)

            @pl.when(live_ref[0] < start + block)
            def _():
                live = lax.broadcasted_iota(jnp.int32, (block, D), 0) + start < live_ref[0]
                k = k_held[keys].astype(jnp.float32)
                first = k_held[:tokens].astype(jnp.float32)[:1]
                k_held[keys] = jnp.where(live, k, first).astype(jnp.bfloat16)
                v = v_held[keys, :D].astype(jnp.float32)
                v_held[keys, :D] = jnp.where(live, v, 0.0).astype(jnp.bfloat16)
                v_held[keys, D:] = jnp.where(live, 1.0, 0.0).astype(jnp.bfloat16)

    base = pl.program_id(0) * per_row
    rows = qkv_ref.shape[2]
    for i in range(per_row):
        q = qkv_ref[base + i, 0]
        stats = stats_ref[base + i]
        total, peak = (
            jnp.transpose(jnp.broadcast_to(stats[j : j + 1], (D, rows))) for j in range(2)
        )
        state = (jnp.concatenate([acc_ref[base + i], total], axis=1), peak[:, :1])
        for step in range(steps):
            keys = slice(step * block, (step + 1) * block)
            state = attend_block(q, k_held[keys], v_held[keys], state)
        out_ref[base + i] = (state[0][:, :D] / state[0][:, D:]).astype(jnp.bfloat16)


def attend_ref(qkv, acc, stats, kv, live):
    shards, _, tokens, _ = qkv.shape
    n = shards * tokens
    n_keys = kv.size // (2 * D)
    return pl.pallas_call(
        functools.partial(ref_kernel, per_row=PER_ROW, steps=2),
        grid=(shards // PER_ROW,),
        in_specs=[whole(pltpu.SMEM)] + [whole()] * 4,
        out_specs=whole(),
        out_shape=jax.ShapeDtypeStruct((shards, tokens, D), jnp.bfloat16),
        scratch_shapes=[
            pltpu.VMEM((n_keys, D), jnp.bfloat16),
            pltpu.VMEM((n_keys, 2 * D), jnp.bfloat16),
        ],
        compiler_params=params(),
        cost_estimate=pl.CostEstimate(
            flops=8 * n * n_keys * D, bytes_accessed=16 * n * D, transcendentals=n * n_keys
        ),
        name="attend_ref",
    )(live, qkv, acc, stats, kv)


def swap(x, axes):
    return lax.all_to_all(x, axes, split_axis=0, concat_axis=0, tiled=True)


def shift_z(piece, shift, n_z):
    if shift == 0:
        return piece
    return lax.ppermute(piece, "z", [(src, (src + shift) % n_z) for src in range(n_z)])


def shards(n_z, queries, keys, values, ref_cache, ref_ids, ref_owner, ref_lens):
    z, x = lax.axis_index("z"), lax.axis_index("x")
    place = jnp.stack([z, x]).astype(jnp.int32)
    live = ref_lens[ref_ids[2 * z + x]].reshape(1)

    cache = ref_cache[0]
    other = lax.dynamic_index_in_dim(cache, 1 - x, 0, keepdims=False)
    other = lax.ppermute(other, "x", [(0, 1), (1, 0)])

    shifts = sorted(range(n_z), key=lambda shift: -min(shift, n_z - shift))
    sent = spread_pieces(n_z, place, shifts, cache, other)

    packed = pack_heads(queries[0], keys[0], values[0])
    packed, sent = lax.optimization_barrier((packed, sent))
    qkv = swap(packed, "sp")
    held = [shift_z(piece, shift, n_z) for piece, shift in zip(sent, shifts)]

    routed = route_pieces(n_z, place, ref_ids, ref_owner, held, shifts)
    tokens = routed.shape[2]
    kv = swap(routed.reshape(-1, tokens, D), ("z", "x", "sp")).reshape(n_z, 2, -1, tokens, D)

    out = attend_ref(qkv, *attend_own(qkv), kv, live)

    back = swap(out, "sp")
    return unpack_heads(back)[None]


def solution(mesh):
    n_grp, n_sp = mesh.devices.shape
    n_z = n_grp // 2
    split = jax.sharding.Mesh(mesh.devices.reshape(n_z, 2, n_sp), ("z", "x", "sp"))
    token_spec = P(("z", "x"), "sp", None)
    return jax.shard_map(
        functools.partial(shards, n_z),
        mesh=split,
        in_specs=(token_spec,) * 3 + (P(("z", "x"), None, "sp", None), P(), P(), P()),
        out_specs=token_spec,
        check_vma=False,
    )
```

```python
import functools
import math

import jax
import jax.numpy as jnp
from jax import lax
from jax.experimental import pallas as pl
from jax.experimental.pallas import tpu as pltpu
from jax.sharding import PartitionSpec as P

D = 128
EXP_SCALE = D**-0.5 * math.log2(math.e)
ROWS_CONTRACT = (((1,), (1,)), ((), ()))
VMEM_LIMIT = 24 << 20
PER_ROW = 8


def params():
    return pltpu.CompilerParams(vmem_limit_bytes=VMEM_LIMIT)


def whole(memory_space=pltpu.VMEM):
    return pl.BlockSpec(memory_space=memory_space)


def pack_kernel(q_ref, k_ref, v_ref, out_ref):
    for head in range(out_ref.shape[0]):
        cols = slice(head * D, (head + 1) * D)
        for which, ref in enumerate((q_ref, k_ref, v_ref)):
            out_ref[head, which] = ref[:, cols]


def pack_heads(q, k, v):
    tokens, width = q.shape
    heads = width // D
    return pl.pallas_call(
        pack_kernel,
        in_specs=[whole()] * 3,
        out_specs=whole(),
        out_shape=jax.ShapeDtypeStruct((heads, 3, tokens, D), q.dtype),
        compiler_params=params(),
        cost_estimate=pl.CostEstimate(flops=0, bytes_accessed=12 * q.size, transcendentals=0),
        name="pack_heads",
    )(q, k, v)


def spread_kernel(n_z, shifts, place_ref, cache_ref, other_ref, *out_refs):
    z, x = place_ref[0], place_ref[1]
    for shift, out_ref in zip(shifts, out_refs):
        tokens = out_ref.shape[1]
        here = pl.ds(pl.multiple_of((z + shift) % n_z * tokens, tokens), tokens)
        out_ref[0] = cache_ref[x, here]
        out_ref[1] = other_ref[here]


def spread_pieces(n_z, place, shifts, cache, other):
    piece = jax.ShapeDtypeStruct((2, cache.shape[1] // n_z, cache.shape[2]), cache.dtype)
    return pl.pallas_call(
        functools.partial(spread_kernel, n_z, shifts),
        in_specs=[whole(pltpu.SMEM), whole(), whole()],
        out_specs=[whole()] * n_z,
        out_shape=[piece] * n_z,
        compiler_params=params(),
        cost_estimate=pl.CostEstimate(flops=0, bytes_accessed=4 * cache.size, transcendentals=0),
        name="spread_pieces",
    )(place, cache, other)


def route_kernel(n_z, shifts, place_ref, ids_ref, owner_ref, *refs):
    out_ref, held = refs[-2:]
    z, x = place_ref[0], place_ref[1]
    for shift, ref in zip(shifts, refs[:-2]):
        held[shift] = ref[0]
        held[n_z + shift] = ref[1]
    for group in range(out_ref.shape[0]):
        row = owner_ref[ids_ref[group]]
        slot = (row + x) % 2 * n_z + (z - row // 2 + n_z) % n_z
        for head in range(out_ref.shape[1]):
            out_ref[group, head] = held[slot, :, head * D : (head + 1) * D]


def route_pieces(n_z, place, ids, owner, pieces, shifts):
    _, tokens, width = pieces[0].shape
    return pl.pallas_call(
        functools.partial(route_kernel, n_z, shifts),
        in_specs=[whole(pltpu.SMEM)] * 3 + [whole()] * len(pieces),
        out_specs=whole(),
        out_shape=jax.ShapeDtypeStruct((2 * n_z, width // D, tokens, D), pieces[0].dtype),
        scratch_shapes=[pltpu.VMEM((2 * n_z, tokens, width), pieces[0].dtype)],
        compiler_params=params(),
        cost_estimate=pl.CostEstimate(
            flops=0, bytes_accessed=8 * n_z * tokens * width, transcendentals=0
        ),
        name="route_pieces",
    )(place, ids, owner, *pieces)


def unpack_kernel(x_ref, out_ref):
    for head in range(x_ref.shape[0]):
        out_ref[:, head * D : (head + 1) * D] = x_ref[head]


def unpack_heads(x):
    heads, tokens, _ = x.shape
    return pl.pallas_call(
        unpack_kernel,
        in_specs=[whole()],
        out_specs=whole(),
        out_shape=jax.ShapeDtypeStruct((tokens, heads * D), x.dtype),
        compiler_params=params(),
        name="unpack_heads",
    )(x)


def attend_block(q, k, v_ones, state):
    s = lax.dot_general(q, k, ROWS_CONTRACT, preferred_element_type=jnp.float32)
    peak = jnp.max(s, axis=1, keepdims=True)
    if state is not None:
        peak = jnp.maximum(state[1], peak)
    p = jnp.exp2((s - peak) * EXP_SCALE).astype(jnp.bfloat16)
    part = jnp.dot(p, v_ones, preferred_element_type=jnp.float32)
    if state is not None:
        part = state[0] * jnp.exp2((state[1] - peak) * EXP_SCALE) + part
    return part, peak


def own_kernel(qkv_ref, acc_ref, stats_ref, *, per_row, steps):
    shards, _, tokens, _ = qkv_ref.shape
    per = shards // steps
    base = pl.program_id(0) * per_row
    for i in range(per_row):
        q = qkv_ref[base + i, 0]
        state = None
        for step in range(steps):
            here = slice(step * per, (step + 1) * per)
            k = qkv_ref[here, 1].reshape(per * tokens, D)
            v = qkv_ref[here, 2].reshape(per * tokens, D)
            v_ones = jnp.concatenate([v, jnp.ones_like(v)], axis=1)
            state = attend_block(q, k, v_ones, state)
        acc_ref[base + i] = state[0][:, :D]
        column = lax.broadcasted_iota(jnp.int32, (tokens, D), 1)
        stats = jnp.where(column == 0, state[0][:, D:], state[1])
        stats_ref[base + i] = jnp.transpose(stats)[: stats_ref.shape[1]]


def attend_own(qkv):
    shards, _, tokens, _ = qkv.shape
    n = shards * tokens
    return pl.pallas_call(
        functools.partial(own_kernel, per_row=PER_ROW, steps=4),
        grid=(shards // PER_ROW,),
        in_specs=[whole()],
        out_specs=[whole()] * 2,
        out_shape=[
            jax.ShapeDtypeStruct((shards, tokens, D), jnp.float32),
            jax.ShapeDtypeStruct((shards, 8, tokens), jnp.float32),
        ],
        compiler_params=params(),
        cost_estimate=pl.CostEstimate(
            flops=8 * n * n * D, bytes_accessed=12 * n * D, transcendentals=n * n
        ),
        name="attend_own",
    )(qkv)


def ref_kernel(
    live_ref, qkv_ref, acc_ref, stats_ref, kv_ref, out_ref, k_held, v_held, *, per_row, steps
):
    pieces, _, shards, tokens, _ = kv_ref.shape
    n_keys = pieces * shards * tokens
    block = n_keys // steps

    @pl.when(pl.program_id(0) == 0)
    def _():
        for piece in range(pieces):
            for shard in range(shards):
                start = (shard * pieces + piece) * tokens
                k_held[start : start + tokens] = kv_ref[piece, 0, shard]
                v_held[start : start + tokens, :D] = kv_ref[piece, 1, shard]
        v_held[:, D:] = jnp.ones((n_keys, D), jnp.bfloat16)

        for start in range(0, n_keys, block):
            keys = slice(start, start + block)

            @pl.when(live_ref[0] < start + block)
            def _():
                live = lax.broadcasted_iota(jnp.int32, (block, D), 0) + start < live_ref[0]
                k = k_held[keys].astype(jnp.float32)
                first = k_held[:tokens].astype(jnp.float32)[:1]
                k_held[keys] = jnp.where(live, k, first).astype(jnp.bfloat16)
                v = v_held[keys, :D].astype(jnp.float32)
                v_held[keys, :D] = jnp.where(live, v, 0.0).astype(jnp.bfloat16)
                v_held[keys, D:] = jnp.where(live, 1.0, 0.0).astype(jnp.bfloat16)

    base = pl.program_id(0) * per_row
    rows = qkv_ref.shape[2]
    for i in range(per_row):
        q = qkv_ref[base + i, 0]
        stats = stats_ref[base + i]
        total, peak = (
            jnp.transpose(jnp.broadcast_to(stats[j : j + 1], (D, rows))) for j in range(2)
        )
        state = (jnp.concatenate([acc_ref[base + i], total], axis=1), peak[:, :1])
        for step in range(steps):
            keys = slice(step * block, (step + 1) * block)
            state = attend_block(q, k_held[keys], v_held[keys], state)
        out_ref[base + i] = (state[0][:, :D] / state[0][:, D:]).astype(jnp.bfloat16)


def attend_ref(qkv, acc, stats, kv, live):
    shards, _, tokens, _ = qkv.shape
    n = shards * tokens
    n_keys = kv.size // (2 * D)
    return pl.pallas_call(
        functools.partial(ref_kernel, per_row=shards, steps=1),
        grid=(1,),
        in_specs=[whole(pltpu.SMEM)] + [whole()] * 4,
        out_specs=whole(),
        out_shape=jax.ShapeDtypeStruct((shards, tokens, D), jnp.bfloat16),
        scratch_shapes=[
            pltpu.VMEM((n_keys, D), jnp.bfloat16),
            pltpu.VMEM((n_keys, 2 * D), jnp.bfloat16),
        ],
        compiler_params=params(),
        cost_estimate=pl.CostEstimate(
            flops=8 * n * n_keys * D, bytes_accessed=16 * n * D, transcendentals=n * n_keys
        ),
        name="attend_ref",
    )(live, qkv, acc, stats, kv)


def swap(x, axes):
    return lax.all_to_all(x, axes, split_axis=0, concat_axis=0, tiled=True)


def shift_z(piece, shift, n_z):
    if shift == 0:
        return piece
    return lax.ppermute(piece, "z", [(src, (src + shift) % n_z) for src in range(n_z)])


def shards(n_z, queries, keys, values, ref_cache, ref_ids, ref_owner, ref_lens):
    z, x = lax.axis_index("z"), lax.axis_index("x")
    place = jnp.stack([z, x]).astype(jnp.int32)
    live = ref_lens[ref_ids[2 * z + x]].reshape(1)

    cache = ref_cache[0]
    other = lax.dynamic_index_in_dim(cache, 1 - x, 0, keepdims=False)
    other = lax.ppermute(other, "x", [(0, 1), (1, 0)])

    shifts = sorted(range(n_z), key=lambda shift: -min(shift, n_z - shift))
    sent = spread_pieces(n_z, place, shifts, cache, other)

    packed = pack_heads(queries[0], keys[0], values[0])
    packed, sent = lax.optimization_barrier((packed, sent))
    qkv = swap(packed, "sp")
    held = [shift_z(piece, shift, n_z) for piece, shift in zip(sent, shifts)]

    routed = route_pieces(n_z, place, ref_ids, ref_owner, held, shifts)
    tokens = routed.shape[2]
    kv = swap(routed.reshape(-1, tokens, D), ("z", "x", "sp")).reshape(n_z, 2, -1, tokens, D)

    out = attend_ref(qkv, *attend_own(qkv), kv, live)

    back = swap(out, "sp")
    return unpack_heads(back)[None]


def solution(mesh):
    n_grp, n_sp = mesh.devices.shape
    n_z = n_grp // 2
    split = jax.sharding.Mesh(mesh.devices.reshape(n_z, 2, n_sp), ("z", "x", "sp"))
    token_spec = P(("z", "x"), "sp", None)
    return jax.shard_map(
        functools.partial(shards, n_z),
        mesh=split,
        in_specs=(token_spec,) * 3 + (P(("z", "x"), None, "sp", None), P(), P(), P()),
        out_specs=token_spec,
        check_vma=False,
    )
```

```python
import functools
import math

import jax
import jax.numpy as jnp
from jax import lax
from jax.experimental import pallas as pl
from jax.experimental.pallas import tpu as pltpu
from jax.sharding import PartitionSpec as P

D = 128
EXP_SCALE = D**-0.5 * math.log2(math.e)
ROWS_CONTRACT = (((1,), (1,)), ((), ()))
VMEM_LIMIT = 24 << 20
PER_ROW = 8


def params():
    return pltpu.CompilerParams(vmem_limit_bytes=VMEM_LIMIT)


def whole(memory_space=pltpu.VMEM):
    return pl.BlockSpec(memory_space=memory_space)


def pack_kernel(q_ref, k_ref, v_ref, out_ref):
    for head in range(out_ref.shape[0]):
        cols = slice(head * D, (head + 1) * D)
        for which, ref in enumerate((q_ref, k_ref, v_ref)):
            out_ref[head, which] = ref[:, cols]


def pack_heads(q, k, v):
    tokens, width = q.shape
    heads = width // D
    return pl.pallas_call(
        pack_kernel,
        in_specs=[whole()] * 3,
        out_specs=whole(),
        out_shape=jax.ShapeDtypeStruct((heads, 3, tokens, D), q.dtype),
        compiler_params=params(),
        cost_estimate=pl.CostEstimate(flops=0, bytes_accessed=12 * q.size, transcendentals=0),
        name="pack_heads",
    )(q, k, v)


def spread_kernel(n_z, shifts, place_ref, cache_ref, other_ref, *out_refs):
    z, x = place_ref[0], place_ref[1]
    for shift, out_ref in zip(shifts, out_refs):
        tokens = out_ref.shape[1]
        here = pl.ds(pl.multiple_of((z + shift) % n_z * tokens, tokens), tokens)
        out_ref[0] = cache_ref[x, here]
        out_ref[1] = other_ref[here]


def spread_pieces(n_z, place, shifts, cache, other):
    piece = jax.ShapeDtypeStruct((2, cache.shape[1] // n_z, cache.shape[2]), cache.dtype)
    return pl.pallas_call(
        functools.partial(spread_kernel, n_z, shifts),
        in_specs=[whole(pltpu.SMEM), whole(), whole()],
        out_specs=[whole()] * n_z,
        out_shape=[piece] * n_z,
        compiler_params=params(),
        cost_estimate=pl.CostEstimate(flops=0, bytes_accessed=4 * cache.size, transcendentals=0),
        name="spread_pieces",
    )(place, cache, other)


def route_kernel(n_z, shifts, place_ref, ids_ref, owner_ref, *refs):
    out_ref, held = refs[-2:]
    z, x = place_ref[0], place_ref[1]
    for shift, ref in zip(shifts, refs[:-2]):
        held[shift] = ref[0]
        held[n_z + shift] = ref[1]
    for group in range(out_ref.shape[0]):
        row = owner_ref[ids_ref[group]]
        slot = (row + x) % 2 * n_z + (z - row // 2 + n_z) % n_z
        for head in range(out_ref.shape[1]):
            out_ref[group, head] = held[slot, :, head * D : (head + 1) * D]


def route_pieces(n_z, place, ids, owner, pieces, shifts):
    _, tokens, width = pieces[0].shape
    return pl.pallas_call(
        functools.partial(route_kernel, n_z, shifts),
        in_specs=[whole(pltpu.SMEM)] * 3 + [whole()] * len(pieces),
        out_specs=whole(),
        out_shape=jax.ShapeDtypeStruct((2 * n_z, width // D, tokens, D), pieces[0].dtype),
        scratch_shapes=[pltpu.VMEM((2 * n_z, tokens, width), pieces[0].dtype)],
        compiler_params=params(),
        cost_estimate=pl.CostEstimate(
            flops=0, bytes_accessed=8 * n_z * tokens * width, transcendentals=0
        ),
        name="route_pieces",
    )(place, ids, owner, *pieces)


def unpack_kernel(x_ref, out_ref):
    for head in range(x_ref.shape[0]):
        out_ref[:, head * D : (head + 1) * D] = x_ref[head]


def unpack_heads(x):
    heads, tokens, _ = x.shape
    return pl.pallas_call(
        unpack_kernel,
        in_specs=[whole()],
        out_specs=whole(),
        out_shape=jax.ShapeDtypeStruct((tokens, heads * D), x.dtype),
        compiler_params=params(),
        name="unpack_heads",
    )(x)


def attend_block(q, k, v_ones, state):
    s = lax.dot_general(q, k, ROWS_CONTRACT, preferred_element_type=jnp.float32)
    peak = jnp.max(s, axis=1, keepdims=True)
    if state is not None:
        peak = jnp.maximum(state[1], peak)
    p = jnp.exp2((s - peak) * EXP_SCALE).astype(jnp.bfloat16)
    part = jnp.dot(p, v_ones, preferred_element_type=jnp.float32)
    if state is not None:
        part = state[0] * jnp.exp2((state[1] - peak) * EXP_SCALE) + part
    return part, peak


def own_kernel(qkv_ref, out_ref, stats_ref, means, *, per_row, steps):
    shards, _, tokens, _ = qkv_ref.shape
    per = shards // steps
    row, rows = pl.program_id(0), shards // per_row

    @pl.when(row < rows)
    def _():
        base = row * per_row
        for i in range(per_row):
            q = qkv_ref[base + i, 0]
            state = None
            for step in range(steps):
                here = slice(step * per, (step + 1) * per)
                k = qkv_ref[here, 1].reshape(per * tokens, D)
                v = qkv_ref[here, 2].reshape(per * tokens, D)
                v_ones = jnp.concatenate([v, jnp.ones_like(v)], axis=1)
                state = attend_block(q, k, v_ones, state)
            mean = state[0][:, :D] / state[0][:, D:]
            high = mean.astype(jnp.bfloat16)
            means[base + i, 0] = high
            means[base + i, 1] = (mean - high.astype(jnp.float32)).astype(jnp.bfloat16)
            column = lax.broadcasted_iota(jnp.int32, (tokens, D), 1)
            stats = jnp.where(column == 0, state[0][:, D:], state[1])
            stats_ref[base + i] = jnp.transpose(stats)[: stats_ref.shape[1]]

    @pl.when(row == rows)
    def _():
        out_ref[:, 0] = qkv_ref[:, 0]
        out_ref[:, 1] = means[:, 0]
        out_ref[:, 2] = means[:, 1]


def attend_own(qkv):
    shards, _, tokens, _ = qkv.shape
    n = shards * tokens
    return pl.pallas_call(
        functools.partial(own_kernel, per_row=PER_ROW, steps=4),
        grid=(shards // PER_ROW + 1,),
        in_specs=[whole()],
        out_specs=[whole()] * 2,
        out_shape=[
            jax.ShapeDtypeStruct(qkv.shape, qkv.dtype),
            jax.ShapeDtypeStruct((shards, 8, tokens), jnp.float32),
        ],
        scratch_shapes=[pltpu.VMEM((shards, 2, tokens, D), jnp.bfloat16)],
        input_output_aliases={0: 0},
        compiler_params=params(),
        cost_estimate=pl.CostEstimate(
            flops=8 * n * n * D, bytes_accessed=12 * n * D, transcendentals=n * n
        ),
        name="attend_own",
    )(qkv)


def ref_kernel(
    live_ref, own_ref, stats_ref, kv_ref, out_ref, k_held, v_held, *, per_row, steps
):
    pieces, _, shards, tokens, _ = kv_ref.shape
    n_keys = pieces * shards * tokens
    block = n_keys // steps

    @pl.when(pl.program_id(0) == 0)
    def _():
        for piece in range(pieces):
            for shard in range(shards):
                start = (shard * pieces + piece) * tokens
                k_held[start : start + tokens] = kv_ref[piece, 0, shard]
                v_held[start : start + tokens, :D] = kv_ref[piece, 1, shard]
        v_held[:, D:] = jnp.ones((n_keys, D), jnp.bfloat16)

        for start in range(0, n_keys, block):
            keys = slice(start, start + block)

            @pl.when(live_ref[0] < start + block)
            def _():
                live = lax.broadcasted_iota(jnp.int32, (block, D), 0) + start < live_ref[0]
                k = k_held[keys].astype(jnp.float32)
                first = k_held[:tokens].astype(jnp.float32)[:1]
                k_held[keys] = jnp.where(live, k, first).astype(jnp.bfloat16)
                v = v_held[keys, :D].astype(jnp.float32)
                v_held[keys, :D] = jnp.where(live, v, 0.0).astype(jnp.bfloat16)
                v_held[keys, D:] = jnp.where(live, 1.0, 0.0).astype(jnp.bfloat16)

    base = pl.program_id(0) * per_row
    rows = own_ref.shape[2]
    for i in range(per_row):
        q = own_ref[base + i, 0]
        stats = stats_ref[base + i]
        total, peak = (
            jnp.transpose(jnp.broadcast_to(stats[j : j + 1], (D, rows))) for j in range(2)
        )
        high, low = (own_ref[base + i, j].astype(jnp.float32) for j in (1, 2))
        state = (jnp.concatenate([(high + low) * total, total], axis=1), peak[:, :1])
        for step in range(steps):
            keys = slice(step * block, (step + 1) * block)
            state = attend_block(q, k_held[keys], v_held[keys], state)
        out_ref[base + i] = (state[0][:, :D] / state[0][:, D:]).astype(jnp.bfloat16)


def attend_ref(own, stats, kv, live):
    shards, _, tokens, _ = own.shape
    n = shards * tokens
    n_keys = kv.size // (2 * D)
    return pl.pallas_call(
        functools.partial(ref_kernel, per_row=shards, steps=1),
        grid=(1,),
        in_specs=[whole(pltpu.SMEM)] + [whole()] * 3,
        out_specs=whole(),
        out_shape=jax.ShapeDtypeStruct((shards, tokens, D), jnp.bfloat16),
        scratch_shapes=[
            pltpu.VMEM((n_keys, D), jnp.bfloat16),
            pltpu.VMEM((n_keys, 2 * D), jnp.bfloat16),
        ],
        compiler_params=params(),
        cost_estimate=pl.CostEstimate(
            flops=8 * n * n_keys * D, bytes_accessed=16 * n * D, transcendentals=n * n_keys
        ),
        name="attend_ref",
    )(live, own, stats, kv)


def swap(x, axes):
    return lax.all_to_all(x, axes, split_axis=0, concat_axis=0, tiled=True)


def shift_z(piece, shift, n_z):
    if shift == 0:
        return piece
    return lax.ppermute(piece, "z", [(src, (src + shift) % n_z) for src in range(n_z)])


def shards(n_z, queries, keys, values, ref_cache, ref_ids, ref_owner, ref_lens):
    z, x = lax.axis_index("z"), lax.axis_index("x")
    place = jnp.stack([z, x]).astype(jnp.int32)
    live = ref_lens[ref_ids[2 * z + x]].reshape(1)

    cache = ref_cache[0]
    other = lax.dynamic_index_in_dim(cache, 1 - x, 0, keepdims=False)
    other = lax.ppermute(other, "x", [(0, 1), (1, 0)])

    shifts = sorted(range(n_z), key=lambda shift: -min(shift, n_z - shift))
    sent = spread_pieces(n_z, place, shifts, cache, other)

    packed = pack_heads(queries[0], keys[0], values[0])
    packed, sent = lax.optimization_barrier((packed, sent))
    qkv = swap(packed, "sp")
    held = [shift_z(piece, shift, n_z) for piece, shift in zip(sent, shifts)]

    routed = route_pieces(n_z, place, ref_ids, ref_owner, held, shifts)
    tokens = routed.shape[2]
    kv = swap(routed.reshape(-1, tokens, D), ("z", "x", "sp")).reshape(n_z, 2, -1, tokens, D)

    out = attend_ref(*attend_own(qkv), kv, live)

    back = swap(out, "sp")
    return unpack_heads(back)[None]


def solution(mesh):
    n_grp, n_sp = mesh.devices.shape
    n_z = n_grp // 2
    split = jax.sharding.Mesh(mesh.devices.reshape(n_z, 2, n_sp), ("z", "x", "sp"))
    token_spec = P(("z", "x"), "sp", None)
    return jax.shard_map(
        functools.partial(shards, n_z),
        mesh=split,
        in_specs=(token_spec,) * 3 + (P(("z", "x"), None, "sp", None), P(), P(), P()),
        out_specs=token_spec,
        check_vma=False,
    )
```

```python
import functools
import math

import jax
import jax.numpy as jnp
from jax import lax
from jax.experimental import pallas as pl
from jax.experimental.pallas import tpu as pltpu
from jax.sharding import PartitionSpec as P

D = 128
EXP_SCALE = D**-0.5 * math.log2(math.e)
ROWS_CONTRACT = (((1,), (1,)), ((), ()))
VMEM_LIMIT = 24 << 20
PER_ROW = 8


def params():
    return pltpu.CompilerParams(vmem_limit_bytes=VMEM_LIMIT)


def whole(memory_space=pltpu.VMEM):
    return pl.BlockSpec(memory_space=memory_space)


def pack_kernel(q_ref, k_ref, v_ref, out_ref):
    for head in range(out_ref.shape[0]):
        cols = slice(head * D, (head + 1) * D)
        for which, ref in enumerate((q_ref, k_ref, v_ref)):
            out_ref[head, which] = ref[:, cols]


def pack_heads(q, k, v):
    tokens, width = q.shape
    heads = width // D
    return pl.pallas_call(
        pack_kernel,
        in_specs=[whole()] * 3,
        out_specs=whole(),
        out_shape=jax.ShapeDtypeStruct((heads, 3, tokens, D), q.dtype),
        compiler_params=params(),
        cost_estimate=pl.CostEstimate(flops=0, bytes_accessed=12 * q.size, transcendentals=0),
        name="pack_heads",
    )(q, k, v)


def spread_kernel(n_z, shifts, place_ref, cache_ref, other_ref, *out_refs):
    z, x = place_ref[0], place_ref[1]
    for shift, out_ref in zip(shifts, out_refs):
        tokens = out_ref.shape[1]
        here = pl.ds(pl.multiple_of((z + shift) % n_z * tokens, tokens), tokens)
        out_ref[0] = cache_ref[x, here]
        out_ref[1] = other_ref[here]


def spread_pieces(n_z, place, shifts, cache, other):
    piece = jax.ShapeDtypeStruct((2, cache.shape[1] // n_z, cache.shape[2]), cache.dtype)
    return pl.pallas_call(
        functools.partial(spread_kernel, n_z, shifts),
        in_specs=[whole(pltpu.SMEM), whole(), whole()],
        out_specs=[whole()] * n_z,
        out_shape=[piece] * n_z,
        compiler_params=params(),
        cost_estimate=pl.CostEstimate(flops=0, bytes_accessed=4 * cache.size, transcendentals=0),
        name="spread_pieces",
    )(place, cache, other)


def route_kernel(n_z, shifts, place_ref, ids_ref, owner_ref, *refs):
    out_ref, held = refs[-2:]
    z, x = place_ref[0], place_ref[1]
    for shift, ref in zip(shifts, refs[:-2]):
        held[shift] = ref[0]
        held[n_z + shift] = ref[1]
    for group in range(out_ref.shape[0]):
        row = owner_ref[ids_ref[group]]
        slot = (row + x) % 2 * n_z + (z - row // 2 + n_z) % n_z
        for head in range(out_ref.shape[1]):
            out_ref[group, head] = held[slot, :, head * D : (head + 1) * D]


def route_pieces(n_z, place, ids, owner, pieces, shifts):
    _, tokens, width = pieces[0].shape
    return pl.pallas_call(
        functools.partial(route_kernel, n_z, shifts),
        in_specs=[whole(pltpu.SMEM)] * 3 + [whole()] * len(pieces),
        out_specs=whole(),
        out_shape=jax.ShapeDtypeStruct((2 * n_z, width // D, tokens, D), pieces[0].dtype),
        scratch_shapes=[pltpu.VMEM((2 * n_z, tokens, width), pieces[0].dtype)],
        compiler_params=params(),
        cost_estimate=pl.CostEstimate(
            flops=0, bytes_accessed=8 * n_z * tokens * width, transcendentals=0
        ),
        name="route_pieces",
    )(place, ids, owner, *pieces)


def unpack_kernel(x_ref, out_ref, sems):
    def move(head):
        columns = out_ref.at[:, head * D : (head + 1) * D]
        return pltpu.make_async_copy(x_ref.at[head], columns, sems.at[head])

    for head in range(x_ref.shape[0]):
        move(head).start()
    for head in range(x_ref.shape[0]):
        move(head).wait()


def unpack_heads(x):
    heads, tokens, _ = x.shape
    return pl.pallas_call(
        unpack_kernel,
        in_specs=[whole()],
        out_specs=whole(pl.ANY),
        out_shape=jax.ShapeDtypeStruct((tokens, heads * D), x.dtype),
        scratch_shapes=[pltpu.SemaphoreType.DMA((heads,))],
        compiler_params=params(),
        name="unpack_heads",
    )(x)


def attend_block(q, k, v_ones, state):
    s = lax.dot_general(q, k, ROWS_CONTRACT, preferred_element_type=jnp.float32)
    peak = jnp.max(s, axis=1, keepdims=True)
    if state is not None:
        peak = jnp.maximum(state[1], peak)
    p = jnp.exp2((s - peak) * EXP_SCALE).astype(jnp.bfloat16)
    part = jnp.dot(p, v_ones, preferred_element_type=jnp.float32)
    if state is not None:
        part = state[0] * jnp.exp2((state[1] - peak) * EXP_SCALE) + part
    return part, peak


def own_kernel(qkv_ref, out_ref, stats_ref, means, *, per_row, steps):
    shards, _, tokens, _ = qkv_ref.shape
    per = shards // steps
    row, rows = pl.program_id(0), shards // per_row

    @pl.when(row < rows)
    def _():
        base = row * per_row
        for i in range(per_row):
            q = qkv_ref[base + i, 0]
            state = None
            for step in range(steps):
                here = slice(step * per, (step + 1) * per)
                k = qkv_ref[here, 1].reshape(per * tokens, D)
                v = qkv_ref[here, 2].reshape(per * tokens, D)
                v_ones = jnp.concatenate([v, jnp.ones_like(v)], axis=1)
                state = attend_block(q, k, v_ones, state)
            mean = state[0][:, :D] / state[0][:, D:]
            high = mean.astype(jnp.bfloat16)
            means[base + i, 0] = high
            means[base + i, 1] = (mean - high.astype(jnp.float32)).astype(jnp.bfloat16)
            column = lax.broadcasted_iota(jnp.int32, (tokens, D), 1)
            stats = jnp.where(column == 0, state[0][:, D:], state[1])
            stats_ref[base + i] = jnp.transpose(stats)[: stats_ref.shape[1]]

    @pl.when(row == rows)
    def _():
        out_ref[:, 0] = qkv_ref[:, 0]
        out_ref[:, 1] = means[:, 0]
        out_ref[:, 2] = means[:, 1]


def attend_own(qkv):
    shards, _, tokens, _ = qkv.shape
    n = shards * tokens
    return pl.pallas_call(
        functools.partial(own_kernel, per_row=PER_ROW, steps=4),
        grid=(shards // PER_ROW + 1,),
        in_specs=[whole()],
        out_specs=[whole()] * 2,
        out_shape=[
            jax.ShapeDtypeStruct(qkv.shape, qkv.dtype),
            jax.ShapeDtypeStruct((shards, 8, tokens), jnp.float32),
        ],
        scratch_shapes=[pltpu.VMEM((shards, 2, tokens, D), jnp.bfloat16)],
        input_output_aliases={0: 0},
        compiler_params=params(),
        cost_estimate=pl.CostEstimate(
            flops=8 * n * n * D, bytes_accessed=12 * n * D, transcendentals=n * n
        ),
        name="attend_own",
    )(qkv)


def ref_kernel(
    live_ref, own_ref, stats_ref, kv_ref, out_ref, k_held, v_held, *, per_row, steps
):
    pieces, _, shards, tokens, _ = kv_ref.shape
    n_keys = pieces * shards * tokens
    block = n_keys // steps

    @pl.when(pl.program_id(0) == 0)
    def _():
        for piece in range(pieces):
            for shard in range(shards):
                start = (shard * pieces + piece) * tokens
                k_held[start : start + tokens] = kv_ref[piece, 0, shard]
                v_held[start : start + tokens, :D] = kv_ref[piece, 1, shard]
        v_held[:, D:] = jnp.ones((n_keys, D), jnp.bfloat16)

        for start in range(0, n_keys, block):
            keys = slice(start, start + block)

            @pl.when(live_ref[0] < start + block)
            def _():
                live = lax.broadcasted_iota(jnp.int32, (block, D), 0) + start < live_ref[0]
                k = k_held[keys].astype(jnp.float32)
                first = k_held[:tokens].astype(jnp.float32)[:1]
                k_held[keys] = jnp.where(live, k, first).astype(jnp.bfloat16)
                v = v_held[keys, :D].astype(jnp.float32)
                v_held[keys, :D] = jnp.where(live, v, 0.0).astype(jnp.bfloat16)
                v_held[keys, D:] = jnp.where(live, 1.0, 0.0).astype(jnp.bfloat16)

    base = pl.program_id(0) * per_row
    rows = own_ref.shape[2]
    for i in range(per_row):
        q = own_ref[base + i, 0]
        stats = stats_ref[base + i]
        total, peak = (
            jnp.transpose(jnp.broadcast_to(stats[j : j + 1], (D, rows))) for j in range(2)
        )
        high, low = (own_ref[base + i, j].astype(jnp.float32) for j in (1, 2))
        state = (jnp.concatenate([(high + low) * total, total], axis=1), peak[:, :1])
        for step in range(steps):
            keys = slice(step * block, (step + 1) * block)
            state = attend_block(q, k_held[keys], v_held[keys], state)
        out_ref[base + i] = (state[0][:, :D] / state[0][:, D:]).astype(jnp.bfloat16)


def attend_ref(own, stats, kv, live):
    shards, _, tokens, _ = own.shape
    n = shards * tokens
    n_keys = kv.size // (2 * D)
    return pl.pallas_call(
        functools.partial(ref_kernel, per_row=shards, steps=1),
        grid=(1,),
        in_specs=[whole(pltpu.SMEM)] + [whole()] * 3,
        out_specs=whole(),
        out_shape=jax.ShapeDtypeStruct((shards, tokens, D), jnp.bfloat16),
        scratch_shapes=[
            pltpu.VMEM((n_keys, D), jnp.bfloat16),
            pltpu.VMEM((n_keys, 2 * D), jnp.bfloat16),
        ],
        compiler_params=params(),
        cost_estimate=pl.CostEstimate(
            flops=8 * n * n_keys * D, bytes_accessed=16 * n * D, transcendentals=n * n_keys
        ),
        name="attend_ref",
    )(live, own, stats, kv)


def swap(x, axes):
    return lax.all_to_all(x, axes, split_axis=0, concat_axis=0, tiled=True)


def shift_z(piece, shift, n_z):
    if shift == 0:
        return piece
    return lax.ppermute(piece, "z", [(src, (src + shift) % n_z) for src in range(n_z)])


def shards(n_z, queries, keys, values, ref_cache, ref_ids, ref_owner, ref_lens):
    z, x = lax.axis_index("z"), lax.axis_index("x")
    place = jnp.stack([z, x]).astype(jnp.int32)
    live = ref_lens[ref_ids[2 * z + x]].reshape(1)

    cache = ref_cache[0]
    other = lax.dynamic_index_in_dim(cache, 1 - x, 0, keepdims=False)
    other = lax.ppermute(other, "x", [(0, 1), (1, 0)])

    shifts = sorted(range(n_z), key=lambda shift: -min(shift, n_z - shift))
    sent = spread_pieces(n_z, place, shifts, cache, other)

    packed = pack_heads(queries[0], keys[0], values[0])
    packed, sent = lax.optimization_barrier((packed, sent))
    qkv = swap(packed, "sp")
    held = [shift_z(piece, shift, n_z) for piece, shift in zip(sent, shifts)]

    routed = route_pieces(n_z, place, ref_ids, ref_owner, held, shifts)
    tokens = routed.shape[2]
    kv = swap(routed.reshape(-1, tokens, D), ("z", "x", "sp")).reshape(n_z, 2, -1, tokens, D)

    out = attend_ref(*attend_own(qkv), kv, live)

    back = swap(out, "sp")
    return unpack_heads(back)[None]


def solution(mesh):
    n_grp, n_sp = mesh.devices.shape
    n_z = n_grp // 2
    split = jax.sharding.Mesh(mesh.devices.reshape(n_z, 2, n_sp), ("z", "x", "sp"))
    token_spec = P(("z", "x"), "sp", None)
    return jax.shard_map(
        functools.partial(shards, n_z),
        mesh=split,
        in_specs=(token_spec,) * 3 + (P(("z", "x"), None, "sp", None), P(), P(), P()),
        out_specs=token_spec,
        check_vma=False,
    )
```
